128 devices in a mesh: dp: 8 (over x, core), fsdp: 16 (over y, z).
Axes of the slice: x: 4, y: 4, z: 4, core: 2. Of those that a mesh axis runs over, the one named last changes fastest.
Arguments:
- hidden_in: bfloat16 [1024, 128, 5120], P(('dp', 'fsdp')), may hold values from -6 to 6
- kv_weight: bfloat16 [5120, 1024], P('fsdp'), may hold values from -0.078125 to 0.078125
- ln_gain: float32 [5120], replicated, may hold values from 0.1 to 1.9
- k_gain: float32 [128], replicated, may hold values from 0.1 to 1.9
- cost_slots: int32 [128, 8], P(('dp', 'fsdp')), may hold values from 0 to 7, each once within a row
- lengths: int32 [1024], P(('dp', 'fsdp')), may hold values from 16 to 128
- rewards: int32 [1024], P(('dp', 'fsdp')), may hold values from 0 to 3
- group_ids: int32 [1024], P(('dp', 'fsdp')), may hold values from 0 to 63, as said below
- kv_cotangent: bfloat16 [1024, 128, 1024], P(('dp', 'fsdp')), may hold values from -16 to 16
Outputs:
- keys_values: bfloat16 [1024, 128, 1024], P(('dp', 'fsdp'))
- kv_grad: float32 [5120, 1024], P('fsdp')
The draws below stay inside these ranges and needn't reach their ends.
Inputs may be any that keep to these rules, and one draw needn't show every extreme that they name: `group_ids`: each prompt has exactly 16 completions.
All inputs are finite; a program needn't handle non-finite values.
Results may differ from the reference program's by a relative error of at most 0.0058.
Values may be sent and summed in bfloat16 or wider, within the bound.
No kernel may reach another device: no remote copies, remote signals or barrier semaphores. Data moves between devices by JAX's collectives and lax.ppermute only.
A program may use at most 192 MiB of HBM per device.

```python
import jax
import jax.numpy as jnp
from jax import lax

D = 5120
HEAD_SIZE = 128
KEY_VALUE_HEADS = 4
COMPLETION_SLOTS = 128
PER_PEER = 1
GROUP = 16
KEY_VALUE_WIDTH = 512
SEQS_DEV = 8
NC = 1024
GROUPS = 64
N_DP = 8
N_FSDP = 16


def draw_group_ids(key, part):
    key = jax.random.fold_in(key, 11)
    shuffled = jax.random.permutation(key, jnp.arange(NC, dtype=jnp.int32))
    return (shuffled // GROUP).astype(jnp.int32)


def touch_ends(drawn, key, smallest, high):
    spot = [jax.random.randint(jax.random.fold_in(key, axis), (), 0, length) for axis, length in enumerate(drawn.shape)]
    widest = drawn.shape.index(max(drawn.shape))
    beside = spot[:widest] + [(spot[widest] + 1) % drawn.shape[widest]] + spot[widest + 1:]
    return drawn.at[tuple(spot)].set(smallest).at[tuple(beside)].set(high)


def block_levels(own_key, dims, split, smallest, top_value):
    factor_of = 1.0
    for dim, parts in split:
        steps = jax.random.uniform(jax.random.fold_in(jax.random.fold_in(own_key, 6), dim), (parts,), jnp.float32, smallest / len(split), top_value / len(split))
        factor_of = factor_of * jnp.repeat(jnp.exp(steps), dims[dim] // parts).reshape((-1,) + (1,) * (len(dims) - 1 - dim))
    return factor_of


def gaussian(rng, dims, deviation, limit, shards=(), held_as=jnp.bfloat16):
    result = jax.random.normal(rng, dims, jnp.float32) * deviation
    if len(shards) > 0:
        result = block_levels(rng, dims, shards, -0.22, 0.18) * result
    return jnp.clip(result, min=-limit, max=limit).astype(held_as)


def setup_inputs(seed: int = 0) -> dict:
    streams_of = jax.random.split(jax.random.key(seed), 10)
    hidden_in = gaussian(streams_of[0], (NC, COMPLETION_SLOTS, D), 1.0, 6.0, ((0, 128),))
    kv_weight = gaussian(streams_of[1], (D, 2 * KEY_VALUE_WIDTH), D ** -0.5, 0.078125, ((0, 16),))
    ln_gain = jnp.clip(1.0 + 0.18 * jax.random.normal(streams_of[2], (D,), jnp.float32), 0.1, 1.9)
    k_gain = jnp.clip(1.0 + 0.18 * jax.random.normal(streams_of[3], (HEAD_SIZE,), jnp.float32), 0.1, 1.9)
    cost_slots = jax.vmap(lambda own: jax.random.permutation(own, SEQS_DEV))(jax.random.split(streams_of[4], (N_DP * N_FSDP))).reshape((N_DP * N_FSDP, SEQS_DEV)).astype(jnp.int32)
    lengths = touch_ends(jax.random.randint(streams_of[5], (NC,), COMPLETION_SLOTS // 8, COMPLETION_SLOTS + 1), jax.random.fold_in(streams_of[5], 1), COMPLETION_SLOTS // 8, COMPLETION_SLOTS).astype(jnp.int32)
    rewards = touch_ends(jax.random.randint(streams_of[6], (NC,), 0, 4), jax.random.fold_in(streams_of[6], 1), 0, 3).astype(jnp.int32)
    group_ids = draw_group_ids(jax.random.fold_in(streams_of[9], 71), 0)
    kv_cotangent = gaussian(streams_of[8], (NC, COMPLETION_SLOTS, 2 * KEY_VALUE_WIDTH), 4.0, 16.0, ((0, 128),))
    return {"hidden_in": hidden_in, "kv_weight": kv_weight, "ln_gain": ln_gain, "k_gain": k_gain, "cost_slots": cost_slots, "lengths": lengths, "rewards": rewards, "group_ids": group_ids, "kv_cotangent": kv_cotangent}


EPS = 1e-06

def rms_scale(values, gain):
    return values * lax.rsqrt(lax.optimization_barrier(jnp.mean(values * values, -1, keepdims=True)) + EPS) * gain

def seq_weights(rewards, group_ids, lengths):
    scores = rewards.astype(jnp.float32)
    member = (group_ids[:, None] == jnp.arange(GROUPS, dtype=jnp.int32)[None, :]).astype(jnp.float32)
    totals = lax.optimization_barrier(jnp.sum(member * scores[:, None], 0))
    squares = lax.optimization_barrier(jnp.sum(member * (scores * scores)[:, None], 0))
    means = totals / GROUP
    spread = squares / GROUP - means * means
    own_mean = lax.optimization_barrier(jnp.sum(member * means[None, :], 1))
    own_spread = lax.optimization_barrier(jnp.sum(member * spread[None, :], 1))
    adv = (scores - own_mean) / jnp.sqrt(jnp.maximum(own_spread, 1.0))
    return adv / lengths.astype(jnp.float32)

def reference(hidden_in, kv_weight, ln_gain, k_gain, cost_slots, lengths, rewards, group_ids, kv_cotangent):
    weight = seq_weights(rewards, group_ids, lengths)
    inv = jnp.argsort(cost_slots, axis=1).astype(jnp.int32)
    source = jnp.arange(N_DP * N_FSDP, dtype=jnp.int32)[:, None] * SEQS_DEV + inv
    order = jnp.transpose(source.reshape(N_DP, N_FSDP, N_DP, PER_PEER), (2, 1, 0, 3)).reshape(NC).astype(jnp.int32)
    positions = jnp.arange(COMPLETION_SLOTS, dtype=jnp.int32)

    def key_norm(keys_before_norm):
        return rms_scale(keys_before_norm, k_gain)

    def step(grad, index):
        anchor = order[index]
        tokens = lax.dynamic_index_in_dim(hidden_in, anchor, 0, False).astype(jnp.float32)
        live = lax.dynamic_index_in_dim(lengths, anchor, 0, False)
        scale = lax.dynamic_index_in_dim(weight, anchor, 0, False)
        coef = jnp.where(positions < live, scale, 0.0).astype(jnp.bfloat16)
        coef = lax.optimization_barrier(coef).astype(jnp.float32)
        normed = rms_scale(tokens, ln_gain).astype(jnp.bfloat16)
        key_value_before_norm = jnp.dot(normed, kv_weight, preferred_element_type=jnp.float32)
        keys_before_norm = key_value_before_norm[:, :KEY_VALUE_WIDTH].reshape(COMPLETION_SLOTS, KEY_VALUE_HEADS, HEAD_SIZE)
        keys, backward_pass = jax.vjp(key_norm, keys_before_norm)
        outputs = jnp.concatenate([keys.reshape(COMPLETION_SLOTS, KEY_VALUE_WIDTH), key_value_before_norm[:, KEY_VALUE_WIDTH:]], 1).astype(jnp.bfloat16)
        incoming_gradient = lax.dynamic_index_in_dim(kv_cotangent, index, 0, False).astype(jnp.float32)
        key_gradient, = backward_pass(incoming_gradient[:, :KEY_VALUE_WIDTH].reshape(COMPLETION_SLOTS, KEY_VALUE_HEADS, HEAD_SIZE))
        scaled = (jnp.concatenate([key_gradient.reshape(COMPLETION_SLOTS, KEY_VALUE_WIDTH), incoming_gradient[:, KEY_VALUE_WIDTH:]], 1) * coef[:, None]).astype(jnp.bfloat16)
        grad = grad + lax.dot_general(normed, scaled, (((0,), (0,)), ((), ())), preferred_element_type=jnp.float32)
        return (grad, outputs)
    grad, keys_values = lax.scan(step, jnp.zeros((D, 2 * KEY_VALUE_WIDTH), jnp.float32), jnp.arange(NC, dtype=jnp.int32))
    return (keys_values, grad)
```

```python
import functools

import jax
import jax.numpy as jnp
from jax import lax
from jax.experimental import pallas as pl
from jax.experimental.pallas import tpu as pltpu
from jax.sharding import PartitionSpec as P

HEAD = 128
GROUP = 16
GROUPS = 64
EPS = 1e-06
SEQS = 8
ROWS = 128
WIDTH = 5120
BLOCK = 320
QUARTER = 1280
HALF = 256
TOKENS = SEQS * ROWS
MIB = 1 << 20

bf16, f32 = jnp.bfloat16, jnp.float32


def ring_yz(dy, dz):
    return [
        (y * 4 + z, ((y + dy) % 4) * 4 + (z + dz) % 4) for y in range(4) for z in range(4)
    ]


def ring_x(dx, flip=0):
    return [(x * 2 + c, ((x + dx) % 4) * 2 + (c ^ flip)) for x in range(4) for c in range(2)]


def along_y(value, step):
    return lax.ppermute(value, "fsdp", ring_yz(step, 0))


def along_z(value, step):
    return lax.ppermute(value, "fsdp", ring_yz(0, step))


def along_x(value, step):
    return lax.ppermute(value, "dp", ring_x(step))


def to_partner(value):
    return lax.ppermute(value, "dp", ring_x(0, 1))


def norm_kernel(order_ref, hidden_ref, gain_ref, rows_ref, columns_ref):
    values = hidden_ref[0].astype(f32)
    mean = jnp.sum(values * values, -1, keepdims=True) * (1.0 / WIDTH)
    normed = (values * lax.rsqrt(mean + EPS) * gain_ref[...]).astype(bf16)
    rows_ref[...] = normed
    columns_ref[...] = normed.T


def norm_call(order, hidden_in, ln_gain):
    return pl.pallas_call(
        norm_kernel,
        grid_spec=pltpu.PrefetchScalarGridSpec(
            num_scalar_prefetch=1,
            grid=(SEQS,),
            in_specs=[
                pl.BlockSpec((1, ROWS, WIDTH), lambda i, o: (o[i], 0, 0)),
                pl.BlockSpec((1, WIDTH), lambda i, o: (0, 0)),
            ],
            out_specs=[
                pl.BlockSpec((ROWS, WIDTH), lambda i, o: (i, 0)),
                pl.BlockSpec((WIDTH, ROWS), lambda i, o: (0, i)),
            ],
        ),
        out_shape=[
            jax.ShapeDtypeStruct((TOKENS, WIDTH), bf16),
            jax.ShapeDtypeStruct((WIDTH, TOKENS), bf16),
        ],
        compiler_params=pltpu.CompilerParams(vmem_limit_bytes=40 * MIB),
        cost_estimate=pl.CostEstimate(
            flops=8 * TOKENS * WIDTH, bytes_accessed=6 * TOKENS * WIDTH, transcendentals=0
        ),
        name="input_norm",
    )(order, hidden_in, ln_gain.reshape(1, WIDTH))


STEP = 512
STEPS = 2 * TOKENS // STEP


def project_kernel(
    place_ref, length_ref, weight_ref, gain_ref, cot_ref, own_ref, partner_ref,
    a0, a1, a2, a3, b0, b1, b2, b3,
    kv_ref, scaled_ref, w_ref, buf_ref, acc_ref, w_sem, buf_sem,
):
    i = pl.program_id(0)
    y, z = place_ref[1], place_ref[2]

    def w_copies():
        out = []
        for k, (a, b) in enumerate(zip((a0, a1, a2, a3), (b0, b1, b2, b3))):
            for r in range(4):
                ya, za = lax.rem(y + 4 - k, 4), lax.rem(z + 4 - r, 4)
                yb, zb = lax.rem(y + 4 - r, 4), lax.rem(z + 4 - k, 4)
                for src, yy, zz, col in ((a, ya, za, 0), (b, yb, zb, HALF)):
                    row = pl.multiple_of((yy * 4 + zz) * BLOCK, BLOCK)
                    out.append(
                        pltpu.make_async_copy(
                            src.at[r], w_ref.at[pl.ds(row, BLOCK), pl.ds(col, HALF)], w_sem
                        )
                    )
        return out

    def block_copy(source, j, slot):
        return pltpu.make_async_copy(
            source.at[pl.ds(pl.multiple_of(j * STEP, STEP), STEP)],
            buf_ref.at[slot],
            buf_sem.at[slot],
        )

    def start_block(j, slot):
        @pl.when(j < STEPS // 2)
        def _():
            block_copy(own_ref, j, slot).start()

        @pl.when(j >= STEPS // 2)
        def _():
            block_copy(partner_ref, j - STEPS // 2, slot).start()

    @pl.when(i == 0)
    def _():
        for copy in w_copies():
            copy.start()
        start_block(0, 0)
        start_block(1, 1)
        for copy in w_copies():
            copy.wait()

    slot = lax.rem(i, 2)
    block_copy(own_ref, 0, slot).wait()

    acc_ref[...] = jnp.dot(buf_ref[slot], w_ref[...], preferred_element_type=f32)

    @pl.when(i + 2 < STEPS)
    def _():
        start_block(i + 2, slot)

    gain = gain_ref[...]
    rows = lax.broadcasted_iota(jnp.int32, (ROWS, 1), 0)
    for q in range(STEP // ROWS):
        n = i * (STEP // ROWS) + q
        coef = jnp.where(rows < length_ref[n], weight_ref[n], 0.0)
        coef = coef.astype(bf16).astype(f32)
        span = pl.ds(q * ROWS, ROWS)
        for head in range(HALF // HEAD):
            columns = pl.ds(head * HEAD, HEAD)
            keys = acc_ref[span, columns]
            scale = lax.rsqrt(jnp.mean(keys * keys, -1, keepdims=True) + EPS)
            unit = keys * scale
            kv_ref[q, 0, :, columns] = (unit * gain).astype(bf16)
            slope = cot_ref[q, 0, :, columns].astype(f32) * gain
            inner = jnp.mean(unit * slope, -1, keepdims=True)
            scaled_ref[span, columns] = ((slope - unit * inner) * scale * coef).astype(bf16)
        columns = pl.ds(HALF, HALF)
        kv_ref[q, 0, :, columns] = acc_ref[span, columns].astype(bf16)
        scaled_ref[span, columns] = (cot_ref[q, 0, :, columns].astype(f32) * coef).astype(bf16)


def project_call(place, lengths, weights, k_gain, cotangent, own, partner, a, b):
    per = STEP // ROWS
    spot = lambda i, p, l, w: (lax.rem(i, 2), lax.rem(lax.div(i, 2) + p[0], 2), 0, 0)
    any_spec = pl.BlockSpec(memory_space=pl.ANY)
    return pl.pallas_call(
        project_kernel,
        grid_spec=pltpu.PrefetchScalarGridSpec(
            num_scalar_prefetch=3,
            grid=(STEPS,),
            in_specs=[
                pl.BlockSpec((1, HEAD), lambda i, p, l, w: (0, 0)),
                pl.BlockSpec((per, 1, ROWS, 2 * HALF), spot),
            ]
            + [any_spec] * 10,
            out_specs=[
                pl.BlockSpec((per, 1, ROWS, 2 * HALF), spot),
                pl.BlockSpec((STEP, 2 * HALF), lambda i, p, l, w: (i, 0)),
            ],
            scratch_shapes=[
                pltpu.VMEM((WIDTH, 2 * HALF), bf16),
                pltpu.VMEM((2, STEP, WIDTH), bf16),
                pltpu.VMEM((STEP, 2 * HALF), f32),
                pltpu.SemaphoreType.DMA,
                pltpu.SemaphoreType.DMA((2,)),
            ],
        ),
        out_shape=[
            jax.ShapeDtypeStruct((SEQS, 2, ROWS, 2 * HALF), bf16),
            jax.ShapeDtypeStruct((2 * TOKENS, 2 * HALF), bf16),
        ],
        compiler_params=pltpu.CompilerParams(vmem_limit_bytes=50 * MIB),
        cost_estimate=pl.CostEstimate(
            flops=4 * TOKENS * WIDTH * 2 * HALF,
            bytes_accessed=4 * TOKENS * WIDTH + 12 * MIB,
            transcendentals=0,
        ),
        name="project",
    )(place, lengths, weights, k_gain.reshape(1, HEAD), cotangent, own, partner, *a, *b)


def gradient_kernel(place_ref, ao_ref, ap_ref, bo_ref, bp_ref, scaled_ref, a_ref, b_ref):
    for own, partner, cols, out in (
        (ao_ref, ap_ref, pl.ds(0, HALF), a_ref),
        (bo_ref, bp_ref, pl.ds(HALF, HALF), b_ref),
    ):
        total = jnp.dot(
            own[0, 0], scaled_ref[pl.ds(0, TOKENS), cols], preferred_element_type=f32
        ) + jnp.dot(
            partner[0, 0], scaled_ref[pl.ds(TOKENS, TOKENS), cols], preferred_element_type=f32
        )
        out[0] = total.astype(bf16)


def gradient_call(step, place, own, partner, scaled):
    def a_spot(i, p):
        return (lax.rem(p[1] + step, 4), lax.rem(p[2] + i, 4), 0, 0)

    def b_spot(i, p):
        return (lax.rem(p[1] + i, 4), lax.rem(p[2] + step, 4), 0, 0)

    block = (1, 1, BLOCK, TOKENS)
    out = pl.BlockSpec((1, BLOCK, HALF), lambda i, p: (i, 0, 0))
    return pl.pallas_call(
        gradient_kernel,
        grid_spec=pltpu.PrefetchScalarGridSpec(
            num_scalar_prefetch=1,
            grid=(4,),
            in_specs=[
                pl.BlockSpec(block, a_spot),
                pl.BlockSpec(block, a_spot),
                pl.BlockSpec(block, b_spot),
                pl.BlockSpec(block, b_spot),
                pl.BlockSpec((2 * TOKENS, 2 * HALF), lambda i, p: (0, 0)),
            ],
            out_specs=[out, out],
        ),
        out_shape=[jax.ShapeDtypeStruct((4, BLOCK, HALF), bf16)] * 2,
        compiler_params=pltpu.CompilerParams(vmem_limit_bytes=40 * MIB),
        cost_estimate=pl.CostEstimate(
            flops=TOKENS * WIDTH * 2 * HALF,
            bytes_accessed=2 * TOKENS * WIDTH + 4 * MIB,
            transcendentals=0,
        ),
        name="weight_gradient",
    )(place, own, partner, own, partner, scaled)


def group_statistics(rewards, group_ids):
    scores = rewards.astype(f32)
    member = (group_ids[:, None] == jnp.arange(GROUPS, dtype=jnp.int32)[None, :]).astype(f32)
    sums = jnp.stack(
        [jnp.sum(member * scores[:, None], 0), jnp.sum(member * (scores * scores)[:, None], 0)]
    ).reshape(1, 1, 2 * GROUPS)
    for axis in ("dp", "fsdp"):
        count = lax.axis_size(axis)
        sums = lax.all_to_all(
            jnp.broadcast_to(sums, (count, 1, 2 * GROUPS)), axis, 0, 0, tiled=True
        ).sum(0, keepdims=True)
    totals, squares = sums[0, 0, :GROUPS], sums[0, 0, GROUPS:]
    means = totals / GROUP
    spread = squares / GROUP - means * means
    own_mean = jnp.sum(member * means[None, :], 1)
    own_spread = jnp.sum(member * spread[None, :], 1)
    return (scores - own_mean) / jnp.sqrt(jnp.maximum(own_spread, 1.0))


def gathered(block, first, second):
    stage = jnp.stack([block, first(block, 1), first(block, 2), first(block, 3)])
    return [stage, second(stage, 1), second(stage, 2), second(stage, 3)]


def on_device(
    hidden_in, kv_weight, ln_gain, k_gain, cost_slots, lengths, rewards, group_ids, kv_cotangent
):
    place_f = lax.axis_index("fsdp")
    y, z = lax.div(place_f, 4), lax.rem(place_f, 4)
    core = lax.rem(lax.axis_index("dp"), 2)
    place = jnp.stack([core, y, z]).astype(jnp.int32)

    by_core = kv_weight.reshape(BLOCK, 2, 2, HALF)
    mine = jnp.where(core == 0, by_core[:, :, 0], by_core[:, :, 1])
    weights_a = gathered(mine[:, 0], along_z, along_y)
    weights_b = gathered(mine[:, 1], along_y, along_z)

    cot_send = (
        kv_cotangent.reshape(4, 2, ROWS, 2, 2, HALF)
        .transpose(0, 4, 1, 2, 3, 5)
        .reshape(SEQS, 2, ROWS, 2 * HALF)
    )
    cot = lax.all_to_all(cot_send, "dp", split_axis=0, concat_axis=0, tiled=True)

    slots = cost_slots[0]
    index = jnp.arange(SEQS, dtype=jnp.int32)
    hit = slots[None, :] == index[:, None]
    order = jnp.sum(jnp.where(hit, index[None, :], 0), 1).astype(jnp.int32)

    normed, normed_t = norm_call(order, hidden_in, ln_gain)
    partner, partner_t = to_partner(normed), to_partner(normed_t)

    weight = group_statistics(rewards, group_ids) / lengths.astype(f32)
    sent = jnp.stack([weight, lengths.astype(f32)])
    sent = jnp.sum(jnp.where(hit[None], sent[:, None, :], 0.0), 2)
    both = jnp.concatenate([sent, to_partner(sent)], 1)

    kv_send, scaled = project_call(
        place, both[1].astype(jnp.int32), both[0], k_gain, cot, normed, partner,
        weights_a, weights_b,
    )

    kv = lax.all_to_all(kv_send, "dp", split_axis=0, concat_axis=0, tiled=True)
    keys_values = (
        kv.reshape(4, 2, 2, ROWS, 2, HALF).transpose(0, 2, 3, 4, 1, 5).reshape(SEQS, ROWS, 4 * HALF)
    )

    own_t = normed_t.reshape(4, 4, BLOCK, TOKENS)
    partner_t = partner_t.reshape(4, 4, BLOCK, TOKENS)
    parts = {k: gradient_call(k, place, own_t, partner_t, scaled) for k in (2, 1, 3, 0)}
    sum_a = sum(along_y(parts[k][0], k).astype(f32) for k in (2, 1, 3)) + parts[0][0].astype(f32)
    sum_b = sum(along_z(parts[k][1], k).astype(f32) for k in (2, 1, 3)) + parts[0][1].astype(f32)
    sum_a = sum(along_z(sum_a[k].astype(bf16), k).astype(f32) for k in (2, 1, 3)) + sum_a[0]
    sum_b = sum(along_y(sum_b[k].astype(bf16), k).astype(f32) for k in (2, 1, 3)) + sum_b[0]
    rows = jnp.stack([sum_a, sum_b], 1)
    rows_sent = rows.astype(bf16)
    ahead = [rows_sent.astype(f32)] + [along_x(rows_sent, k).astype(f32) for k in (1, 2, 3)]
    rows = (ahead[0] + ahead[2]) + (ahead[1] + ahead[3])
    other = to_partner(rows)
    kv_grad = jnp.where(
        core == 0, jnp.stack([rows, other], 2), jnp.stack([other, rows], 2)
    ).reshape(BLOCK, 4 * HALF)
    return keys_values, kv_grad


def solution(mesh):
    in_specs = (
        P(("dp", "fsdp"), None, None),
        P("fsdp", None),
        P(),
        P(),
        P(("dp", "fsdp"), None),
        P(("dp", "fsdp")),
        P(("dp", "fsdp")),
        P(("dp", "fsdp")),
        P(("dp", "fsdp"), None, None),
    )
    out_specs = (P(("dp", "fsdp"), None, None), P("fsdp", None))
    return jax.shard_map(
        on_device, mesh=mesh, in_specs=in_specs, out_specs=out_specs, check_vma=False
    )
```

```python
import jax
import jax.numpy as jnp
from jax import lax
from jax.experimental import pallas as pl
from jax.experimental.pallas import tpu as pltpu
from jax.sharding import PartitionSpec as P

HEAD = 128
GROUP = 16
GROUPS = 64
EPS = 1e-06
SEQS = 8
ROWS = 128
WIDTH = 5120
BLOCK = 320
PAIR = 2 * BLOCK
HALF = 256
COLS = 2 * HALF
TOKENS = SEQS * ROWS
MIB = 1 << 20
BOTH = ("dp", "fsdp")

bf16, f32 = jnp.bfloat16, jnp.float32
COST = pl.CostEstimate(flops=1, bytes_accessed=1, transcendentals=0)


def along(value, long_axis, flip):
    pairs = []
    for dp in range(8):
        for y in range(4):
            for z in range(4):
                there = (y ^ flip) * 4 + z if (dp % 2 == 0) == long_axis else y * 4 + (z ^ flip)
                pairs.append((dp * 16 + y * 4 + z, dp * 16 + there))
    return lax.ppermute(value, BOTH, pairs)


def along_x(value, flip):
    return lax.ppermute(value, "dp", [(i, i ^ (2 * flip)) for i in range(8)])


def to_partner(value):
    return lax.ppermute(value, "dp", [(i, i ^ 1) for i in range(8)])


def params():
    return pltpu.CompilerParams(vmem_limit_bytes=48 * MIB)


def window(pair_of, j, place):
    pair = pair_of(place)
    return jnp.where(place[0] == 0, 4 * pair + j, 2 * j + pair)


def own_pair(place):
    return lax.div(place[1], 2)


def other_pair(place):
    return 1 - lax.div(place[1], 2)


def scale_kernel(hidden_ref, scale_ref):
    values = hidden_ref[0].astype(f32)
    mean = jnp.sum(values * values, -1, keepdims=True) * (1.0 / WIDTH)
    scale_ref[...] = jnp.broadcast_to(lax.rsqrt(mean + EPS), (ROWS, HEAD))


def scale_call(hidden):
    return pl.pallas_call(
        scale_kernel,
        grid=(SEQS,),
        in_specs=[pl.BlockSpec((1, ROWS, WIDTH), lambda i: (i, 0, 0))],
        out_specs=pl.BlockSpec((ROWS, HEAD), lambda i: (i, 0)),
        out_shape=jax.ShapeDtypeStruct((TOKENS, HEAD), f32),
        compiler_params=params(),
        cost_estimate=COST,
        name="token_scale",
    )(hidden)


SEQ_STEP = 4
STEP = SEQ_STEP * ROWS


def load_weights(place, pieces, w_ref, sem):
    u, v = place[1], place[2]
    first = pl.program_id(0) == 0
    for m, piece in enumerate(pieces):
        for n in range(4):
            bit, vv = lax.rem(u + m, 2), lax.bitwise_xor(v, n)
            row = jnp.where(place[0] == 0, bit * 4 + vv, vv * 2 + bit) * BLOCK
            copy = pltpu.make_async_copy(
                piece.at[pl.ds(n * BLOCK, BLOCK)],
                w_ref.at[pl.ds(pl.multiple_of(row, BLOCK), BLOCK)],
                sem,
            )
            pl.when(first)(copy.start)

    @pl.when(first)
    def _():
        for piece in pieces:
            for n in range(4):
                span = pl.ds(n * BLOCK, BLOCK)
                pltpu.make_async_copy(piece.at[span], w_ref.at[span], sem).wait()


def product(refs, w_ref):
    values = jnp.concatenate([ref[...].reshape(STEP, PAIR) for ref in refs], 1)
    return jnp.dot(values, w_ref[...], preferred_element_type=f32)


def first_kernel(place, *refs):
    own, partner, pieces, (sum_ref, w_ref, sem) = refs[:4], refs[4:8], refs[8:10], refs[10:]
    load_weights(place, pieces, w_ref, sem)
    sum_ref[0] = product(own, w_ref)
    sum_ref[1] = product(partner, w_ref)


def group_of(totals, group):
    lane = lax.broadcasted_iota(jnp.int32, (1, 2 * GROUPS), 1)
    mean, square = (
        jnp.sum(jnp.where(lane == group + k * GROUPS, totals, 0.0), -1, keepdims=True) / GROUP
        for k in range(2)
    )
    return mean, square - mean * mean


def second_kernel(place, facts, *refs):
    own, partner, pieces = refs[:4], refs[4:8], refs[8:10]
    (
        totals_ref, sum_ref, cot_own, cot_partner, scale_own, scale_partner, gain_ref,
        kv_ref, scaled_ref, w_ref, pre_ref, sem,
    ) = refs[10:]
    load_weights(place, pieces, w_ref, sem)
    gain = gain_ref[...]
    totals = totals_ref[...]
    rows = lax.broadcasted_iota(jnp.int32, (ROWS, HEAD), 0)
    i = pl.program_id(0)
    for side, (tokens, cot_ref, scale_ref) in enumerate(
        ((own, cot_own, scale_own), (partner, cot_partner, scale_partner))
    ):
        pre_ref[...] = product(tokens, w_ref) + sum_ref[side]
        for q in range(SEQ_STEP):
            n = i * SEQ_STEP + q
            slot, live, reward, group = (facts[4 * side + k, n] for k in range(4))
            span = pl.ds(q * ROWS, ROWS)
            mean, spread = group_of(totals, group)
            weight = (reward.astype(f32) - mean) / jnp.sqrt(jnp.maximum(spread, 1.0))
            weight = weight / jnp.full((1, 1), live, jnp.int32).astype(f32)
            coef = jnp.where(rows < live, weight, 0.0).astype(bf16).astype(f32)
            scale = scale_ref[span]
            coef = coef * scale
            for part in range(COLS // HEAD):
                columns = pl.ds(part * HEAD, HEAD)
                values = pre_ref[span, columns] * scale
                cot = cot_ref[slot, :, columns].astype(f32)
                if part < HALF // HEAD:
                    root = lax.rsqrt(jnp.mean(values * values, -1, keepdims=True) + EPS)
                    unit = values * root
                    kv_ref[slot, side, :, columns] = (unit * gain).astype(bf16)
                    slope = cot * gain
                    inner = jnp.mean(unit * slope, -1, keepdims=True)
                    cot = (slope - unit * inner) * root
                else:
                    kv_ref[slot, side, :, columns] = values.astype(bf16)
                scaled_ref[side, span, columns] = (cot * coef).astype(bf16)


def token_specs(pair_of):
    return [
        pl.BlockSpec(
            (SEQ_STEP, ROWS, PAIR), lambda i, p, *s, j=j: (i, 0, window(pair_of, j, p))
        )
        for j in range(4)
    ] * 2


ANY_SPEC = pl.BlockSpec(memory_space=pl.ANY)
SUM_SPEC = pl.BlockSpec((2, STEP, COLS), lambda i, *s: (0, i, 0))
W_SCRATCH = pltpu.VMEM((4 * PAIR, COLS), bf16)


def first_call(place, own, partner, weights):
    return pl.pallas_call(
        first_kernel,
        grid_spec=pltpu.PrefetchScalarGridSpec(
            num_scalar_prefetch=1,
            grid=(TOKENS // STEP,),
            in_specs=token_specs(own_pair) + [ANY_SPEC] * 2,
            out_specs=SUM_SPEC,
            scratch_shapes=[W_SCRATCH, pltpu.SemaphoreType.DMA],
        ),
        out_shape=jax.ShapeDtypeStruct((2, TOKENS, COLS), f32),
        compiler_params=params(),
        cost_estimate=COST,
        name="project_first",
    )(place, *[own] * 4, *[partner] * 4, *weights)


def second_call(place, facts, totals, own, partner, weights, sums, cots, scales, k_gain):
    whole = pl.BlockSpec((SEQS, ROWS, COLS), lambda i, *s: (0, 0, 0))
    wide = pl.BlockSpec((STEP, HEAD), lambda i, *s: (i, 0))
    return pl.pallas_call(
        second_kernel,
        grid_spec=pltpu.PrefetchScalarGridSpec(
            num_scalar_prefetch=2,
            grid=(TOKENS // STEP,),
            in_specs=token_specs(other_pair)
            + [ANY_SPEC] * 2
            + [pl.BlockSpec((1, 2 * GROUPS), lambda i, *s: (0, 0))]
            + [SUM_SPEC, whole, whole, wide, wide]
            + [pl.BlockSpec((1, HEAD), lambda i, *s: (0, 0))],
            out_specs=[
                pl.BlockSpec((SEQS, 2, ROWS, COLS), lambda i, *s: (0, 0, 0, 0)),
                SUM_SPEC,
            ],
            scratch_shapes=[W_SCRATCH, pltpu.VMEM((STEP, COLS), f32), pltpu.SemaphoreType.DMA],
        ),
        out_shape=[
            jax.ShapeDtypeStruct((SEQS, 2, ROWS, COLS), bf16),
            jax.ShapeDtypeStruct((2, TOKENS, COLS), bf16),
        ],
        compiler_params=params(),
        cost_estimate=COST,
        name="project_second",
    )(
        place, facts, *[own] * 4, *[partner] * 4, *weights, totals, sums, *cots, *scales,
        k_gain.reshape(1, HEAD),
    )


def gradient_kernel(place, own_ref, partner_ref, scaled_ref, same_ref, cross_ref):
    core, u, v = place[0], place[1], place[2]
    j = pl.program_id(0)
    total = None
    for side, ref in enumerate((own_ref, partner_ref)):
        part = lax.dot_general(
            ref[...].reshape(TOKENS, PAIR),
            scaled_ref[side],
            (((0,), (0,)), ((), ())),
            preferred_element_type=f32,
        )
        total = part if total is None else total + part
    total = total.astype(bf16)
    for s in range(2):
        bit = jnp.where(core == 0, lax.div(j, 2), s)
        vv = jnp.where(core == 0, 2 * lax.rem(j, 2) + s, j)
        n = lax.bitwise_xor(vv, v)
        rows = total[s * BLOCK : (s + 1) * BLOCK]
        same = bit == lax.rem(u, 2)

        @pl.when(same)
        def _():
            same_ref[n] = rows

        @pl.when(jnp.logical_not(same))
        def _():
            cross_ref[n] = rows


def gradient_call(pair_of, place, own, partner, scaled):
    tokens = pl.BlockSpec((SEQS, ROWS, PAIR), lambda j, p: (0, 0, window(pair_of, j, p)))
    out = pl.BlockSpec((4, BLOCK, COLS), lambda j, p: (0, 0, 0))
    return pl.pallas_call(
        gradient_kernel,
        grid_spec=pltpu.PrefetchScalarGridSpec(
            num_scalar_prefetch=1,
            grid=(4,),
            in_specs=[tokens, tokens, pl.BlockSpec((2, TOKENS, COLS), lambda j, p: (0, 0, 0))],
            out_specs=[out, out],
        ),
        out_shape=[jax.ShapeDtypeStruct((4, BLOCK, COLS), bf16)] * 2,
        compiler_params=params(),
        cost_estimate=COST,
        name="weight_gradient",
    )(place, own, partner, scaled)


def group_sums(rewards, group_ids):
    scores = rewards.astype(f32)
    member = (group_ids[:, None] == jnp.arange(GROUPS, dtype=jnp.int32)[None, :]).astype(f32)
    return jnp.concatenate(
        [jnp.sum(member * scores[:, None], 0), jnp.sum(member * (scores * scores)[:, None], 0)]
    ).reshape(1, 1, 2 * GROUPS)


def summed_over(sums, axis):
    sums = jnp.broadcast_to(sums, (lax.axis_size(axis), 1, 2 * GROUPS))
    return lax.all_to_all(sums, axis, 0, 0, tiled=True).sum(0, keepdims=True)


def columns_of(core, array):
    k0, k1, v0, v1 = (array[..., i * HALF : (i + 1) * HALF] for i in range(4))
    return jnp.where(
        core == 0, jnp.concatenate([k0, v0], -1), jnp.concatenate([k1, v1], -1)
    )


def all_columns(core, mine, other):
    low, high = jnp.where(core == 0, mine, other), jnp.where(core == 0, other, mine)
    return jnp.concatenate(
        [low[..., :HALF], high[..., :HALF], low[..., HALF:], high[..., HALF:]], -1
    )


def on_device(
    hidden_in, kv_weight, ln_gain, k_gain, cost_slots, lengths, rewards, group_ids, kv_cotangent
):
    place_f = lax.axis_index("fsdp")
    core = lax.rem(lax.axis_index("dp"), 2)
    y, z = lax.div(place_f, 4), lax.rem(place_f, 4)
    place = jnp.stack([core, jnp.where(core == 0, y, z), jnp.where(core == 0, z, y)])
    place = place.astype(jnp.int32)
    gain = lax.dynamic_slice(ln_gain, (place_f * BLOCK,), (BLOCK,))[:, None]

    facts = jnp.stack([cost_slots[0], lengths, rewards, group_ids])
    facts = jnp.concatenate([facts, to_partner(facts)])

    mine = (columns_of(core, kv_weight).astype(f32) * gain).astype(bf16)
    totals = summed_over(group_sums(rewards, group_ids), "dp")
    piece = jnp.concatenate([mine] + [along(mine, False, n) for n in (1, 2, 3)])
    pieces = [piece] + [along(piece, True, m) for m in (1, 2, 3)]

    kv_cotangent, _ = lax.optimization_barrier((kv_cotangent, totals))
    cot = lax.all_to_all(kv_cotangent, "dp", split_axis=0, concat_axis=0, tiled=True)
    swapped, totals, _ = lax.optimization_barrier((hidden_in, totals, piece))
    partner = to_partner(swapped)
    totals = summed_over(totals, "fsdp").reshape(1, 2 * GROUPS)

    scale = scale_call(hidden_in)
    cot, scale, totals = lax.optimization_barrier((cot, scale, totals))
    cots = columns_of(core, cot), to_partner(columns_of(1 - core, cot))

    scales = scale, to_partner(scale)
    sums = first_call(place, hidden_in, partner, pieces[:2])
    kv, scaled = second_call(
        place, facts, totals, hidden_in, partner, pieces[2:], sums, cots, scales, k_gain
    )
    kv = lax.all_to_all(kv, "dp", split_axis=0, concat_axis=0, tiled=True)

    two, three = gradient_call(other_pair, place, hidden_in, partner, scaled)
    here, one = gradient_call(own_pair, place, hidden_in, partner, scaled)
    total = (
        here.astype(f32)
        + along(two, True, 2).astype(f32)
        + along(three, True, 3).astype(f32)
        + along(one, True, 1).astype(f32)
    )
    total = sum(along(total[n].astype(bf16), False, n).astype(f32) for n in (2, 1, 3)) + total[0]
    rows = total.astype(bf16)
    kv, rows = lax.optimization_barrier((kv, rows))
    kv = kv.reshape(4, 2, 2, ROWS, COLS)
    low, high = kv[:, 0], jnp.stack([kv[:, 1, 1], kv[:, 1, 0]], 1)
    keys_values = jnp.concatenate(
        [low[..., :HALF], high[..., :HALF], low[..., HALF:], high[..., HALF:]], -1
    ).reshape(SEQS, ROWS, 2 * COLS)
    ring = [rows.astype(f32)] + [along_x(rows, k).astype(f32) for k in (1, 2, 3)]
    rows = ((ring[0] + ring[2]) + (ring[1] + ring[3])) * gain
    rows, keys_values = lax.optimization_barrier((rows, keys_values))
    return keys_values, all_columns(core, rows, to_partner(rows))


def solution(mesh):
    in_specs = (
        P(("dp", "fsdp"), None, None),
        P("fsdp", None),
        P(),
        P(),
        P(("dp", "fsdp"), None),
        P(("dp", "fsdp")),
        P(("dp", "fsdp")),
        P(("dp", "fsdp")),
        P(("dp", "fsdp"), None, None),
    )
    out_specs = (P(("dp", "fsdp"), None, None), P("fsdp", None))
    return jax.shard_map(
        on_device, mesh=mesh, in_specs=in_specs, out_specs=out_specs, check_vma=False
    )
```

```python
import jax
import jax.numpy as jnp
from jax import lax
from jax.experimental import pallas as pl
from jax.experimental.pallas import tpu as pltpu
from jax.sharding import PartitionSpec as P

HEAD = 128
GROUP = 16
GROUPS = 64
EPS = 1e-06
SEQS = 8
ROWS = 128
WIDTH = 5120
BLOCK = 320
PAIR = 2 * BLOCK
HALF = 256
COLS = 2 * HALF
TOKENS = SEQS * ROWS
EXTRA = 16
MIB = 1 << 20
BOTH = ("dp", "fsdp")

bf16, f32 = jnp.bfloat16, jnp.float32
COST = pl.CostEstimate(flops=1, bytes_accessed=1, transcendentals=0)


def along(value, long_axis, flip):
    pairs = []
    for dp in range(8):
        for y in range(4):
            for z in range(4):
                there = (y ^ flip) * 4 + z if (dp % 2 == 0) == long_axis else y * 4 + (z ^ flip)
                pairs.append((dp * 16 + y * 4 + z, dp * 16 + there))
    return lax.ppermute(value, BOTH, pairs)


def along_x(value, flip):
    return lax.ppermute(value, "dp", [(i, i ^ (2 * flip)) for i in range(8)])


def to_partner(value):
    return lax.ppermute(value, "dp", [(i, i ^ 1) for i in range(8)])


def params():
    return pltpu.CompilerParams(vmem_limit_bytes=48 * MIB)


def window(pair_of, j, place):
    pair = pair_of(place)
    return jnp.where(place[0] == 0, 4 * pair + j, 2 * j + pair)


def own_pair(place):
    return lax.div(place[1], 2)


def other_pair(place):
    return 1 - lax.div(place[1], 2)


def scale_kernel(hidden_ref, scale_ref):
    values = hidden_ref[0].astype(f32)
    mean = jnp.sum(values * values, -1, keepdims=True) * (1.0 / WIDTH)
    scale_ref[...] = jnp.broadcast_to(lax.rsqrt(mean + EPS), (ROWS, HEAD))


def scale_call(hidden):
    return pl.pallas_call(
        scale_kernel,
        grid=(SEQS,),
        in_specs=[pl.BlockSpec((1, ROWS, WIDTH), lambda i: (i, 0, 0))],
        out_specs=pl.BlockSpec((ROWS, HEAD), lambda i: (i, 0)),
        out_shape=jax.ShapeDtypeStruct((TOKENS, HEAD), f32),
        compiler_params=params(),
        cost_estimate=COST,
        name="token_scale",
    )(hidden)


SEQ_STEP = 4
STEP = SEQ_STEP * ROWS


def load_weights(place, pieces, w_ref, sem):
    u, v = place[1], place[2]
    first = pl.program_id(0) == 0
    for m, piece in enumerate(pieces):
        for n in range(4):
            bit, vv = lax.rem(u + m, 2), lax.bitwise_xor(v, n)
            row = jnp.where(place[0] == 0, bit * 4 + vv, vv * 2 + bit) * BLOCK
            copy = pltpu.make_async_copy(
                piece.at[pl.ds(n * BLOCK, BLOCK)],
                w_ref.at[pl.ds(pl.multiple_of(row, BLOCK), BLOCK)],
                sem,
            )
            pl.when(first)(copy.start)

    @pl.when(first)
    def _():
        for piece in pieces:
            for n in range(4):
                span = pl.ds(n * BLOCK, BLOCK)
                pltpu.make_async_copy(piece.at[span], w_ref.at[span], sem).wait()


def product(refs, w_ref):
    values = jnp.concatenate([ref[...].reshape(STEP, PAIR) for ref in refs], 1)
    return jnp.dot(values, w_ref[...], preferred_element_type=f32)


def first_kernel(place, *refs):
    own, partner, pieces, (sum_ref, w_ref, sem) = refs[:4], refs[4:8], refs[8:10], refs[10:]
    load_weights(place, pieces, w_ref, sem)
    sum_ref[0] = product(own, w_ref)
    sum_ref[1] = product(partner, w_ref)


def group_of(totals, group):
    lane = lax.broadcasted_iota(jnp.int32, (1, 2 * GROUPS), 1)
    mean, square = (
        jnp.sum(jnp.where(lane == group + k * GROUPS, totals, 0.0), -1, keepdims=True) / GROUP
        for k in range(2)
    )
    return mean, square - mean * mean


def second_kernel(place, facts, *refs):
    own, partner, pieces = refs[:4], refs[4:8], refs[8:10]
    (
        sum_ref, cot_ref, scale_own, scale_partner, gain_ref,
        kv_ref, scaled_ref, w_ref, pre_ref, sem,
    ) = refs[10:]
    load_weights(place, pieces, w_ref, sem)
    gain = gain_ref[...]
    totals = sum(cot_ref[d, 0, ROWS : ROWS + 1, : 2 * GROUPS].astype(f32) for d in range(SEQS))
    rows = lax.broadcasted_iota(jnp.int32, (ROWS, HEAD), 0)
    i = pl.program_id(0)
    for side, (tokens, scale_ref) in enumerate(((own, scale_own), (partner, scale_partner))):
        source = lax.bitwise_xor(place[0], side)
        pre_ref[side] = product(tokens, w_ref) + sum_ref[side]
        for q in range(SEQ_STEP):
            n = i * SEQ_STEP + q
            slot, live, reward, group = (facts[4 * side + k, n] for k in range(4))
            span = pl.ds(q * ROWS, ROWS)
            mean, spread = group_of(totals, group)
            weight = (reward.astype(f32) - mean) / jnp.sqrt(jnp.maximum(spread, 1.0))
            weight = weight / jnp.full((1, 1), live, jnp.int32).astype(f32)
            coef = jnp.where(rows < live, weight, 0.0).astype(bf16).astype(f32)
            scale = scale_ref[span]
            coef = coef * scale
            for part in range(COLS // HEAD):
                columns = pl.ds(part * HEAD, HEAD)
                values = pre_ref[side, span, columns] * scale
                cot = cot_ref[slot, source, 0:ROWS, columns].astype(f32)
                if part < HALF // HEAD:
                    root = lax.rsqrt(jnp.mean(values * values, -1, keepdims=True) + EPS)
                    unit = values * root
                    kv_ref[slot, side, :, columns] = (unit * gain).astype(bf16)
                    slope = cot * gain
                    inner = jnp.mean(unit * slope, -1, keepdims=True)
                    cot = (slope - unit * inner) * root
                else:
                    kv_ref[slot, side, :, columns] = values.astype(bf16)
                scaled_ref[side, span, columns] = (cot * coef).astype(bf16)


def token_specs(pair_of):
    return [
        pl.BlockSpec(
            (SEQ_STEP, ROWS, PAIR), lambda i, p, *s, j=j: (i, 0, window(pair_of, j, p))
        )
        for j in range(4)
    ] * 2


ANY_SPEC = pl.BlockSpec(memory_space=pl.ANY)
SUM_SPEC = pl.BlockSpec((2, STEP, COLS), lambda i, *s: (0, i, 0))
W_SCRATCH = pltpu.VMEM((4 * PAIR, COLS), bf16)


def first_call(place, own, partner, weights):
    return pl.pallas_call(
        first_kernel,
        grid_spec=pltpu.PrefetchScalarGridSpec(
            num_scalar_prefetch=1,
            grid=(TOKENS // STEP,),
            in_specs=token_specs(own_pair) + [ANY_SPEC] * 2,
            out_specs=SUM_SPEC,
            scratch_shapes=[W_SCRATCH, pltpu.SemaphoreType.DMA],
        ),
        out_shape=jax.ShapeDtypeStruct((2, TOKENS, COLS), f32),
        compiler_params=params(),
        cost_estimate=COST,
        name="project_first",
    )(place, *[own] * 4, *[partner] * 4, *weights)


def second_call(place, facts, own, partner, weights, sums, cot, scales, k_gain):
    whole = pl.BlockSpec((SEQS, 2, ROWS, COLS), lambda i, *s: (0, 0, 0, 0))
    cots = pl.BlockSpec((SEQS, 2, ROWS + EXTRA, COLS), lambda i, *s: (0, 0, 0, 0))
    wide = pl.BlockSpec((STEP, HEAD), lambda i, *s: (i, 0))
    return pl.pallas_call(
        second_kernel,
        grid_spec=pltpu.PrefetchScalarGridSpec(
            num_scalar_prefetch=2,
            grid=(TOKENS // STEP,),
            in_specs=token_specs(other_pair)
            + [ANY_SPEC] * 2
            + [SUM_SPEC, cots, wide, wide]
            + [pl.BlockSpec((1, HEAD), lambda i, *s: (0, 0))],
            out_specs=[whole, SUM_SPEC],
            scratch_shapes=[W_SCRATCH, pltpu.VMEM((2, STEP, COLS), f32), pltpu.SemaphoreType.DMA],
        ),
        out_shape=[
            jax.ShapeDtypeStruct((SEQS, 2, ROWS, COLS), bf16),
            jax.ShapeDtypeStruct((2, TOKENS, COLS), bf16),
        ],
        compiler_params=params(),
        cost_estimate=COST,
        name="project_second",
    )(
        place, facts, *[own] * 4, *[partner] * 4, *weights, sums, cot, *scales,
        k_gain.reshape(1, HEAD),
    )


def gradient_kernel(place, own_ref, partner_ref, scaled_ref, same_ref, cross_ref):
    core, u, v = place[0], place[1], place[2]
    j = pl.program_id(0)
    total = None
    for side, ref in enumerate((own_ref, partner_ref)):
        part = lax.dot_general(
            ref[...].reshape(TOKENS, PAIR),
            scaled_ref[side],
            (((0,), (0,)), ((), ())),
            preferred_element_type=f32,
        )
        total = part if total is None else total + part
    total = total.astype(bf16)
    for s in range(2):
        bit = jnp.where(core == 0, lax.div(j, 2), s)
        vv = jnp.where(core == 0, 2 * lax.rem(j, 2) + s, j)
        n = lax.bitwise_xor(vv, v)
        rows = total[s * BLOCK : (s + 1) * BLOCK]
        same = bit == lax.rem(u, 2)

        @pl.when(same)
        def _():
            same_ref[n] = rows

        @pl.when(jnp.logical_not(same))
        def _():
            cross_ref[n] = rows


def gradient_call(pair_of, place, own, partner, scaled):
    tokens = pl.BlockSpec((SEQS, ROWS, PAIR), lambda j, p: (0, 0, window(pair_of, j, p)))
    out = pl.BlockSpec((4, BLOCK, COLS), lambda j, p: (0, 0, 0))
    return pl.pallas_call(
        gradient_kernel,
        grid_spec=pltpu.PrefetchScalarGridSpec(
            num_scalar_prefetch=1,
            grid=(4,),
            in_specs=[tokens, tokens, pl.BlockSpec((2, TOKENS, COLS), lambda j, p: (0, 0, 0))],
            out_specs=[out, out],
        ),
        out_shape=[jax.ShapeDtypeStruct((4, BLOCK, COLS), bf16)] * 2,
        compiler_params=params(),
        cost_estimate=COST,
        name="weight_gradient",
    )(place, own, partner, scaled)


def group_sums(rewards, group_ids):
    scores = rewards.astype(f32)
    member = (group_ids[:, None] == jnp.arange(GROUPS, dtype=jnp.int32)[None, :]).astype(f32)
    return jnp.concatenate(
        [jnp.sum(member * scores[:, None], 0), jnp.sum(member * (scores * scores)[:, None], 0)]
    ).reshape(1, 2 * GROUPS)


def as_rows(sums):
    return jnp.pad(sums.astype(bf16), ((0, EXTRA - 1), (0, COLS - 2 * GROUPS)))


def columns_of(core, array):
    k0, k1, v0, v1 = (array[..., i * HALF : (i + 1) * HALF] for i in range(4))
    return jnp.where(
        core == 0, jnp.concatenate([k0, v0], -1), jnp.concatenate([k1, v1], -1)
    )


def all_columns(core, mine, other):
    low, high = jnp.where(core == 0, mine, other), jnp.where(core == 0, other, mine)
    return jnp.concatenate(
        [low[..., :HALF], high[..., :HALF], low[..., HALF:], high[..., HALF:]], -1
    )


def on_device(
    hidden_in, kv_weight, ln_gain, k_gain, cost_slots, lengths, rewards, group_ids, kv_cotangent
):
    place_f = lax.axis_index("fsdp")
    core = lax.rem(lax.axis_index("dp"), 2)
    y, z = lax.div(place_f, 4), lax.rem(place_f, 4)
    place = jnp.stack([core, jnp.where(core == 0, y, z), jnp.where(core == 0, z, y)])
    place = place.astype(jnp.int32)
    gain = lax.dynamic_slice(ln_gain, (place_f * BLOCK,), (BLOCK,))[:, None]

    facts = jnp.stack([cost_slots[0], lengths, rewards, group_ids])
    facts = jnp.concatenate([facts, to_partner(facts)])

    mine = (columns_of(core, kv_weight).astype(f32) * gain).astype(bf16)
    sums = group_sums(rewards, group_ids)
    sums = sums + sum(along(sums, True, m) for m in (1, 2, 3))
    mine = jnp.concatenate([mine, as_rows(sums)])
    blocks = [mine] + [along(mine, False, n) for n in (1, 2, 3)]
    piece = jnp.concatenate([block[:BLOCK] for block in blocks])
    pieces = [piece] + [along(piece, True, m) for m in (1, 2, 3)]

    totals = sum(block[BLOCK : BLOCK + 1, : 2 * GROUPS].astype(f32) for block in blocks)

    k0, k1, v0, v1 = (
        kv_cotangent[..., i * HALF : (i + 1) * HALF].reshape(4, 2, ROWS, HALF) for i in range(4)
    )
    cot = jnp.stack([jnp.concatenate([k0, v0], -1), jnp.concatenate([k1, v1], -1)], 1)
    totals = jnp.broadcast_to(as_rows(totals), (SEQS, 2, EXTRA, COLS))
    cot = jnp.concatenate([cot.reshape(SEQS, 2, ROWS, COLS), totals], 2)
    cot = lax.all_to_all(cot, "dp", split_axis=0, concat_axis=0, tiled=True)

    swapped, _ = lax.optimization_barrier((hidden_in, piece))
    partner = to_partner(swapped)

    scale = scale_call(hidden_in)

    scales = scale, to_partner(scale)
    sums = first_call(place, hidden_in, partner, pieces[:2])
    kv, scaled = second_call(
        place, facts, hidden_in, partner, pieces[2:], sums, cot, scales, k_gain
    )
    kv = lax.all_to_all(kv, "dp", split_axis=0, concat_axis=0, tiled=True)

    two, three = gradient_call(other_pair, place, hidden_in, partner, scaled)
    here, one = gradient_call(own_pair, place, hidden_in, partner, scaled)
    total = (
        here.astype(f32)
        + along(two, True, 2).astype(f32)
        + along(three, True, 3).astype(f32)
        + along(one, True, 1).astype(f32)
    )
    total = sum(along(total[n].astype(bf16), False, n).astype(f32) for n in (2, 1, 3)) + total[0]
    rows = total.astype(bf16)
    kv, rows = lax.optimization_barrier((kv, rows))
    kv = kv.reshape(4, 2, 2, ROWS, COLS)
    low, high = kv[:, 0], jnp.stack([kv[:, 1, 1], kv[:, 1, 0]], 1)
    keys_values = jnp.concatenate(
        [low[..., :HALF], high[..., :HALF], low[..., HALF:], high[..., HALF:]], -1
    ).reshape(SEQS, ROWS, 2 * COLS)
    ring = [rows.astype(f32)] + [along_x(rows, k).astype(f32) for k in (1, 2, 3)]
    rows = ((ring[0] + ring[2]) + (ring[1] + ring[3])) * gain
    rows, keys_values = lax.optimization_barrier((rows, keys_values))
    return keys_values, all_columns(core, rows, to_partner(rows))


def solution(mesh):
    in_specs = (
        P(("dp", "fsdp"), None, None),
        P("fsdp", None),
        P(),
        P(),
        P(("dp", "fsdp"), None),
        P(("dp", "fsdp")),
        P(("dp", "fsdp")),
        P(("dp", "fsdp")),
        P(("dp", "fsdp"), None, None),
    )
    out_specs = (P(("dp", "fsdp"), None, None), P("fsdp", None))
    return jax.shard_map(
        on_device, mesh=mesh, in_specs=in_specs, out_specs=out_specs, check_vma=False
    )
```

```python
import jax
import jax.numpy as jnp
from jax import lax
from jax.experimental import pallas as pl
from jax.experimental.pallas import tpu as pltpu
from jax.sharding import PartitionSpec as P

HEAD = 128
GROUP = 16
GROUPS = 64
EPS = 1e-06
SEQS = 8
ROWS = 128
WIDTH = 5120
BLOCK = 320
PAIR = 2 * BLOCK
HALF = 256
COLS = 2 * HALF
TOKENS = SEQS * ROWS
EXTRA = 16
MIB = 1 << 20
BOTH = ("dp", "fsdp")

bf16, f32 = jnp.bfloat16, jnp.float32
COST = pl.CostEstimate(flops=1, bytes_accessed=1, transcendentals=0)


def along(value, long_axis, flip):
    pairs = []
    for dp in range(8):
        for y in range(4):
            for z in range(4):
                there = (y ^ flip) * 4 + z if (dp % 2 == 0) == long_axis else y * 4 + (z ^ flip)
                pairs.append((dp * 16 + y * 4 + z, dp * 16 + there))
    return lax.ppermute(value, BOTH, pairs)


def along_x(value, flip):
    return lax.ppermute(value, "dp", [(i, i ^ (2 * flip)) for i in range(8)])


def to_partner(value):
    return lax.ppermute(value, "dp", [(i, i ^ 1) for i in range(8)])


def params():
    return pltpu.CompilerParams(vmem_limit_bytes=48 * MIB)


def window(pair_of, j, place):
    pair = pair_of(place)
    return jnp.where(place[0] == 0, 4 * pair + j, 2 * j + pair)


def own_pair(place):
    return lax.div(place[1], 2)


def other_pair(place):
    return 1 - lax.div(place[1], 2)


def scale_kernel(hidden_ref, scale_ref):
    values = hidden_ref[0].astype(f32)
    mean = jnp.sum(values * values, -1, keepdims=True) * (1.0 / WIDTH)
    scale_ref[...] = jnp.broadcast_to(lax.rsqrt(mean + EPS), (ROWS, HEAD))


def scale_call(hidden):
    return pl.pallas_call(
        scale_kernel,
        grid=(SEQS,),
        in_specs=[pl.BlockSpec((1, ROWS, WIDTH), lambda i: (i, 0, 0))],
        out_specs=pl.BlockSpec((ROWS, HEAD), lambda i: (i, 0)),
        out_shape=jax.ShapeDtypeStruct((TOKENS, HEAD), f32),
        compiler_params=params(),
        cost_estimate=COST,
        name="token_scale",
    )(hidden)


SEQ_STEP = 2
STEP = SEQ_STEP * ROWS


def load_weights(place, pieces, w_ref, sem):
    u, v = place[1], place[2]
    first = pl.program_id(0) == 0
    for m, piece in enumerate(pieces):
        for n in range(4):
            bit, vv = lax.rem(u + m, 2), lax.bitwise_xor(v, n)
            row = jnp.where(place[0] == 0, bit * 4 + vv, vv * 2 + bit) * BLOCK
            copy = pltpu.make_async_copy(
                piece.at[pl.ds(n * BLOCK, BLOCK)],
                w_ref.at[pl.ds(pl.multiple_of(row, BLOCK), BLOCK)],
                sem,
            )
            pl.when(first)(copy.start)

    @pl.when(first)
    def _():
        for piece in pieces:
            for n in range(4):
                span = pl.ds(n * BLOCK, BLOCK)
                pltpu.make_async_copy(piece.at[span], w_ref.at[span], sem).wait()


def product(refs, w_ref):
    values = jnp.concatenate([ref[...].reshape(STEP, PAIR) for ref in refs], 1)
    return jnp.dot(values, w_ref[...], preferred_element_type=f32)


def first_kernel(place, *refs):
    own, partner, pieces, (sum_ref, w_ref, sem) = refs[:4], refs[4:8], refs[8:10], refs[10:]
    load_weights(place, pieces, w_ref, sem)
    sum_ref[0] = product(own, w_ref)
    sum_ref[1] = product(partner, w_ref)


def group_of(totals, group):
    lane = lax.broadcasted_iota(jnp.int32, (1, 2 * GROUPS), 1)
    mean, square = (
        jnp.sum(jnp.where(lane == group + k * GROUPS, totals, 0.0), -1, keepdims=True) / GROUP
        for k in range(2)
    )
    return mean, square - mean * mean


def second_kernel(place, facts, *refs):
    own, partner, pieces = refs[:4], refs[4:8], refs[8:10]
    (
        sum_ref, cot_ref, scale_own, scale_partner, gain_ref,
        kv_ref, scaled_ref, w_ref, pre_ref, sem,
    ) = refs[10:]
    load_weights(place, pieces, w_ref, sem)
    gain = gain_ref[...]
    totals = sum(cot_ref[d, 0, ROWS : ROWS + 1, : 2 * GROUPS].astype(f32) for d in range(SEQS))
    rows = lax.broadcasted_iota(jnp.int32, (ROWS, HEAD), 0)
    i = pl.program_id(0)
    for side, (tokens, scale_ref) in enumerate(((own, scale_own), (partner, scale_partner))):
        source = lax.bitwise_xor(place[0], side)
        pre_ref[side] = product(tokens, w_ref) + sum_ref[side]
        for q in range(SEQ_STEP):
            n = i * SEQ_STEP + q
            slot, live, reward, group = (facts[4 * side + k, n] for k in range(4))
            span = pl.ds(q * ROWS, ROWS)
            mean, spread = group_of(totals, group)
            weight = (reward.astype(f32) - mean) / jnp.sqrt(jnp.maximum(spread, 1.0))
            weight = weight / jnp.full((1, 1), live, jnp.int32).astype(f32)
            coef = jnp.where(rows < live, weight, 0.0).astype(bf16).astype(f32)
            scale = scale_ref[span]
            coef = coef * scale
            for part in range(COLS // HEAD):
                columns = pl.ds(part * HEAD, HEAD)
                values = pre_ref[side, span, columns] * scale
                cot = cot_ref[slot, source, 0:ROWS, columns].astype(f32)
                if part < HALF // HEAD:
                    root = lax.rsqrt(jnp.mean(values * values, -1, keepdims=True) + EPS)
                    unit = values * root
                    kv_ref[slot, side, :, columns] = (unit * gain).astype(bf16)
                    slope = cot * gain
                    inner = jnp.mean(unit * slope, -1, keepdims=True)
                    cot = (slope - unit * inner) * root
                else:
                    kv_ref[slot, side, :, columns] = values.astype(bf16)
                scaled_ref[side, span, columns] = (cot * coef).astype(bf16)


def token_specs(pair_of):
    return [
        pl.BlockSpec(
            (SEQ_STEP, ROWS, PAIR), lambda i, p, *s, j=j: (i, 0, window(pair_of, j, p))
        )
        for j in range(4)
    ] * 2


ANY_SPEC = pl.BlockSpec(memory_space=pl.ANY)
SUM_SPEC = pl.BlockSpec((2, STEP, COLS), lambda i, *s: (0, i, 0))
W_SCRATCH = pltpu.VMEM((4 * PAIR, COLS), bf16)


def first_call(place, own, partner, weights):
    return pl.pallas_call(
        first_kernel,
        grid_spec=pltpu.PrefetchScalarGridSpec(
            num_scalar_prefetch=1,
            grid=(TOKENS // STEP,),
            in_specs=token_specs(own_pair) + [ANY_SPEC] * 2,
            out_specs=SUM_SPEC,
            scratch_shapes=[W_SCRATCH, pltpu.SemaphoreType.DMA],
        ),
        out_shape=jax.ShapeDtypeStruct((2, TOKENS, COLS), f32),
        compiler_params=params(),
        cost_estimate=COST,
        name="project_first",
    )(place, *[own] * 4, *[partner] * 4, *weights)


def second_call(place, facts, own, partner, weights, sums, cot, scales, k_gain):
    whole = pl.BlockSpec((SEQS, 2, ROWS, COLS), lambda i, *s: (0, 0, 0, 0))
    cots = pl.BlockSpec((SEQS, 2, ROWS + EXTRA, COLS), lambda i, *s: (0, 0, 0, 0))
    wide = pl.BlockSpec((STEP, HEAD), lambda i, *s: (i, 0))
    return pl.pallas_call(
        second_kernel,
        grid_spec=pltpu.PrefetchScalarGridSpec(
            num_scalar_prefetch=2,
            grid=(TOKENS // STEP,),
            in_specs=token_specs(other_pair)
            + [ANY_SPEC] * 2
            + [SUM_SPEC, cots, wide, wide]
            + [pl.BlockSpec((1, HEAD), lambda i, *s: (0, 0))],
            out_specs=[whole, SUM_SPEC],
            scratch_shapes=[W_SCRATCH, pltpu.VMEM((2, STEP, COLS), f32), pltpu.SemaphoreType.DMA],
        ),
        out_shape=[
            jax.ShapeDtypeStruct((SEQS, 2, ROWS, COLS), bf16),
            jax.ShapeDtypeStruct((2, TOKENS, COLS), bf16),
        ],
        compiler_params=params(),
        cost_estimate=COST,
        name="project_second",
    )(
        place, facts, *[own] * 4, *[partner] * 4, *weights, sums, cot, *scales,
        k_gain.reshape(1, HEAD),
    )


def gradient_kernel(place, own_ref, partner_ref, scaled_ref, same_ref, cross_ref):
    core, u, v = place[0], place[1], place[2]
    j = pl.program_id(0)
    total = None
    for side, ref in enumerate((own_ref, partner_ref)):
        part = lax.dot_general(
            ref[...].reshape(TOKENS, PAIR),
            scaled_ref[side],
            (((0,), (0,)), ((), ())),
            preferred_element_type=f32,
        )
        total = part if total is None else total + part
    total = total.astype(bf16)
    for s in range(2):
        bit = jnp.where(core == 0, lax.div(j, 2), s)
        vv = jnp.where(core == 0, 2 * lax.rem(j, 2) + s, j)
        n = lax.bitwise_xor(vv, v)
        rows = total[s * BLOCK : (s + 1) * BLOCK]
        same = bit == lax.rem(u, 2)

        @pl.when(same)
        def _():
            same_ref[n] = rows

        @pl.when(jnp.logical_not(same))
        def _():
            cross_ref[n] = rows


def gradient_call(pair_of, place, own, partner, scaled):
    tokens = pl.BlockSpec((SEQS, ROWS, PAIR), lambda j, p: (0, 0, window(pair_of, j, p)))
    out = pl.BlockSpec((4, BLOCK, COLS), lambda j, p: (0, 0, 0))
    return pl.pallas_call(
        gradient_kernel,
        grid_spec=pltpu.PrefetchScalarGridSpec(
            num_scalar_prefetch=1,
            grid=(4,),
            in_specs=[tokens, tokens, pl.BlockSpec((2, TOKENS, COLS), lambda j, p: (0, 0, 0))],
            out_specs=[out, out],
        ),
        out_shape=[jax.ShapeDtypeStruct((4, BLOCK, COLS), bf16)] * 2,
        compiler_params=params(),
        cost_estimate=COST,
        name="weight_gradient",
    )(place, own, partner, scaled)


def sums_kernel(rewards_ref, groups_ref, sums_ref):
    lane = lax.broadcasted_iota(jnp.int32, (1, 2 * GROUPS), 1)
    total = jnp.zeros((1, 2 * GROUPS), jnp.int32)
    for n in range(SEQS):
        reward, group = rewards_ref[n], groups_ref[n]
        total += jnp.where(lane == group, reward, 0)
        total += jnp.where(lane == group + GROUPS, reward * reward, 0)
    sums_ref[...] = total.astype(f32)


def group_sums(rewards, group_ids):
    return pl.pallas_call(
        sums_kernel,
        in_specs=[pl.BlockSpec(memory_space=pltpu.SMEM)] * 2,
        out_specs=pl.BlockSpec(memory_space=pltpu.VMEM),
        out_shape=jax.ShapeDtypeStruct((1, 2 * GROUPS), f32),
        cost_estimate=COST,
        name="group_sums",
    )(rewards, group_ids)


def as_rows(sums):
    return jnp.pad(sums.astype(bf16), ((0, EXTRA - 1), (0, COLS - 2 * GROUPS)))


def columns_of(core, array):
    k0, k1, v0, v1 = (array[..., i * HALF : (i + 1) * HALF] for i in range(4))
    return jnp.where(
        core == 0, jnp.concatenate([k0, v0], -1), jnp.concatenate([k1, v1], -1)
    )


def all_columns(core, mine, other):
    low, high = jnp.where(core == 0, mine, other), jnp.where(core == 0, other, mine)
    return jnp.concatenate(
        [low[..., :HALF], high[..., :HALF], low[..., HALF:], high[..., HALF:]], -1
    )


def on_device(
    hidden_in, kv_weight, ln_gain, k_gain, cost_slots, lengths, rewards, group_ids, kv_cotangent
):
    place_f = lax.axis_index("fsdp")
    core = lax.rem(lax.axis_index("dp"), 2)
    y, z = lax.div(place_f, 4), lax.rem(place_f, 4)
    place = jnp.stack([core, jnp.where(core == 0, y, z), jnp.where(core == 0, z, y)])
    place = place.astype(jnp.int32)
    gain = lax.dynamic_slice(ln_gain, (place_f * BLOCK,), (BLOCK,))[:, None]

    facts = jnp.stack([cost_slots[0], lengths, rewards, group_ids])
    facts = jnp.concatenate([facts, to_partner(facts)])

    mine = (columns_of(core, kv_weight).astype(f32) * gain).astype(bf16)
    sums = group_sums(rewards, group_ids)
    sums = sums + sum(along(sums, True, m) for m in (1, 2, 3))
    mine = jnp.concatenate([mine, as_rows(sums)])
    blocks = [mine] + [along(mine, False, n) for n in (1, 2, 3)]
    piece = jnp.concatenate([block[:BLOCK] for block in blocks])
    pieces = [piece] + [along(piece, True, m) for m in (1, 2, 3)]

    totals = sum(block[BLOCK : BLOCK + 1, : 2 * GROUPS].astype(f32) for block in blocks)

    k0, k1, v0, v1 = (
        kv_cotangent[..., i * HALF : (i + 1) * HALF].reshape(4, 2, ROWS, HALF) for i in range(4)
    )
    cot = jnp.stack([jnp.concatenate([k0, v0], -1), jnp.concatenate([k1, v1], -1)], 1)
    totals = jnp.broadcast_to(as_rows(totals), (SEQS, 2, EXTRA, COLS))
    cot = jnp.concatenate([cot.reshape(SEQS, 2, ROWS, COLS), totals], 2)
    cot = lax.all_to_all(cot, "dp", split_axis=0, concat_axis=0, tiled=True)

    swapped, _ = lax.optimization_barrier((hidden_in, piece))
    partner = to_partner(swapped)

    scale = scale_call(hidden_in)

    scales = scale, to_partner(scale)
    sums = first_call(place, hidden_in, partner, pieces[:2])
    kv, scaled = second_call(
        place, facts, hidden_in, partner, pieces[2:], sums, cot, scales, k_gain
    )
    kv = lax.all_to_all(kv, "dp", split_axis=0, concat_axis=0, tiled=True)

    two, three = gradient_call(other_pair, place, hidden_in, partner, scaled)
    here, one = gradient_call(own_pair, place, hidden_in, partner, scaled)
    received = [here, along(two, True, 2), along(three, True, 3), along(one, True, 1)]
    total = None
    for n in (2, 1, 3, 0):
        block = sum(part[n].astype(f32) for part in received)
        if n:
            received = lax.optimization_barrier(received)
            block = along(block.astype(bf16), False, n).astype(f32)
        total = block if total is None else total + block
    rows = total.astype(bf16)
    kv, rows = lax.optimization_barrier((kv, rows))
    kv = kv.reshape(4, 2, 2, ROWS, COLS)
    low, high = kv[:, 0], jnp.stack([kv[:, 1, 1], kv[:, 1, 0]], 1)
    keys_values = jnp.concatenate(
        [low[..., :HALF], high[..., :HALF], low[..., HALF:], high[..., HALF:]], -1
    ).reshape(SEQS, ROWS, 2 * COLS)
    ring = [rows.astype(f32)] + [along_x(rows, k).astype(f32) for k in (1, 2, 3)]
    rows = ((ring[0] + ring[2]) + (ring[1] + ring[3])) * gain
    rows, keys_values = lax.optimization_barrier((rows, keys_values))
    return keys_values, all_columns(core, rows, to_partner(rows))


def solution(mesh):
    in_specs = (
        P(("dp", "fsdp"), None, None),
        P("fsdp", None),
        P(),
        P(),
        P(("dp", "fsdp"), None),
        P(("dp", "fsdp")),
        P(("dp", "fsdp")),
        P(("dp", "fsdp")),
        P(("dp", "fsdp"), None, None),
    )
    out_specs = (P(("dp", "fsdp"), None, None), P("fsdp", None))
    return jax.shard_map(
        on_device, mesh=mesh, in_specs=in_specs, out_specs=out_specs, check_vma=False
    )
```

```python
import jax
import jax.numpy as jnp
from jax import lax
from jax.experimental import pallas as pl
from jax.experimental.pallas import tpu as pltpu
from jax.sharding import PartitionSpec as P

HEAD = 128
GROUP = 16
GROUPS = 64
EPS = 1e-06
SEQS = 8
ROWS = 128
WIDTH = 5120
BLOCK = 320
PAIR = 2 * BLOCK
HALF = 256
COLS = 2 * HALF
TOKENS = SEQS * ROWS
EXTRA = 16
MIB = 1 << 20
BOTH = ("dp", "fsdp")

bf16, f32 = jnp.bfloat16, jnp.float32
COST = pl.CostEstimate(flops=1, bytes_accessed=1, transcendentals=0)


def along(value, long_axis, flip):
    pairs = []
    for dp in range(8):
        for y in range(4):
            for z in range(4):
                there = (y ^ flip) * 4 + z if (dp % 2 == 0) == long_axis else y * 4 + (z ^ flip)
                pairs.append((dp * 16 + y * 4 + z, dp * 16 + there))
    return lax.ppermute(value, BOTH, pairs)


def along_x(value, flip):
    return lax.ppermute(value, "dp", [(i, i ^ (2 * flip)) for i in range(8)])


def to_partner(value):
    return lax.ppermute(value, "dp", [(i, i ^ 1) for i in range(8)])


def params(mib=48):
    return pltpu.CompilerParams(vmem_limit_bytes=mib * MIB)


def window(pair_of, j, place):
    pair = pair_of(place)
    return jnp.where(place[0] == 0, 4 * pair + j, 2 * j + pair)


def own_pair(place):
    return lax.div(place[1], 2)


def other_pair(place):
    return 1 - lax.div(place[1], 2)


def scale_kernel(hidden_ref, scale_ref):
    values = hidden_ref[0].astype(f32)
    mean = jnp.sum(values * values, -1, keepdims=True) * (1.0 / WIDTH)
    scale_ref[...] = jnp.broadcast_to(lax.rsqrt(mean + EPS), (ROWS, HEAD))


def scale_call(hidden):
    return pl.pallas_call(
        scale_kernel,
        grid=(SEQS,),
        in_specs=[pl.BlockSpec((1, ROWS, WIDTH), lambda i: (i, 0, 0))],
        out_specs=pl.BlockSpec((ROWS, HEAD), lambda i: (i, 0)),
        out_shape=jax.ShapeDtypeStruct((TOKENS, HEAD), f32),
        compiler_params=params(),
        cost_estimate=COST,
        name="token_scale",
    )(hidden)


SEQ_STEP = 2
STEP = SEQ_STEP * ROWS


def load_weights(place, pieces, w_ref, sem):
    u, v = place[1], place[2]
    first = pl.program_id(0) == 0
    for m, piece in enumerate(pieces):
        for n in range(4):
            bit, vv = lax.rem(u + m, 2), lax.bitwise_xor(v, n)
            row = jnp.where(place[0] == 0, bit * 4 + vv, vv * 2 + bit) * BLOCK
            copy = pltpu.make_async_copy(
                piece.at[pl.ds(n * BLOCK, BLOCK)],
                w_ref.at[pl.ds(pl.multiple_of(row, BLOCK), BLOCK)],
                sem,
            )
            pl.when(first)(copy.start)

    @pl.when(first)
    def _():
        for piece in pieces:
            for n in range(4):
                span = pl.ds(n * BLOCK, BLOCK)
                pltpu.make_async_copy(piece.at[span], w_ref.at[span], sem).wait()


def product(refs, w_ref):
    values = jnp.concatenate([ref[...].reshape(STEP, PAIR) for ref in refs], 1)
    return jnp.dot(values, w_ref[...], preferred_element_type=f32)


def first_kernel(place, *refs):
    own, partner, pieces, (sum_ref, w_ref, sem) = refs[:4], refs[4:8], refs[8:10], refs[10:]
    load_weights(place, pieces, w_ref, sem)
    sum_ref[0] = product(own, w_ref)
    sum_ref[1] = product(partner, w_ref)


def group_of(totals, group):
    lane = lax.broadcasted_iota(jnp.int32, (1, 2 * GROUPS), 1)
    mean, square = (
        jnp.sum(jnp.where(lane == group + k * GROUPS, totals, 0.0), -1, keepdims=True) / GROUP
        for k in range(2)
    )
    return mean, square - mean * mean


def second_kernel(place, facts, *refs):
    own, partner, pieces = refs[:4], refs[4:8], refs[8:10]
    (
        sum_ref, cot_ref, scale_own, scale_partner, gain_ref,
        kv_ref, scaled_ref, w_ref, pre_ref, sem,
    ) = refs[10:]
    load_weights(place, pieces, w_ref, sem)
    gain = gain_ref[...]
    totals = sum(cot_ref[d, 0, ROWS : ROWS + 1, : 2 * GROUPS].astype(f32) for d in range(SEQS))
    rows = lax.broadcasted_iota(jnp.int32, (ROWS, HEAD), 0)
    i = pl.program_id(0)
    for side, (tokens, scale_ref) in enumerate(((own, scale_own), (partner, scale_partner))):
        source = lax.bitwise_xor(place[0], side)
        pre_ref[side] = product(tokens, w_ref) + sum_ref[side]
        for q in range(SEQ_STEP):
            n = i * SEQ_STEP + q
            slot, live, reward, group = (facts[4 * side + k, n] for k in range(4))
            span = pl.ds(q * ROWS, ROWS)
            mean, spread = group_of(totals, group)
            weight = (reward.astype(f32) - mean) / jnp.sqrt(jnp.maximum(spread, 1.0))
            weight = weight / jnp.full((1, 1), live, jnp.int32).astype(f32)
            coef = jnp.where(rows < live, weight, 0.0).astype(bf16).astype(f32)
            scale = scale_ref[span]
            coef = coef * scale
            for part in range(COLS // HEAD):
                columns = pl.ds(part * HEAD, HEAD)
                values = pre_ref[side, span, columns] * scale
                cot = cot_ref[slot, source, 0:ROWS, columns].astype(f32)
                if part < HALF // HEAD:
                    root = lax.rsqrt(jnp.mean(values * values, -1, keepdims=True) + EPS)
                    unit = values * root
                    kv_ref[slot, side, :, columns] = (unit * gain).astype(bf16)
                    slope = cot * gain
                    inner = jnp.mean(unit * slope, -1, keepdims=True)
                    cot = (slope - unit * inner) * root
                else:
                    kv_ref[slot, side, :, columns] = values.astype(bf16)
                scaled_ref[side, span, columns] = (cot * coef).astype(bf16)


def token_specs(pair_of):
    return [
        pl.BlockSpec(
            (SEQ_STEP, ROWS, PAIR), lambda i, p, *s, j=j: (i, 0, window(pair_of, j, p))
        )
        for j in range(4)
    ] * 2


ANY_SPEC = pl.BlockSpec(memory_space=pl.ANY)
SUM_SPEC = pl.BlockSpec((2, STEP, COLS), lambda i, *s: (0, i, 0))
W_SCRATCH = pltpu.VMEM((4 * PAIR, COLS), bf16)


def first_call(place, own, partner, weights):
    return pl.pallas_call(
        first_kernel,
        grid_spec=pltpu.PrefetchScalarGridSpec(
            num_scalar_prefetch=1,
            grid=(TOKENS // STEP,),
            in_specs=token_specs(own_pair) + [ANY_SPEC] * 2,
            out_specs=SUM_SPEC,
            scratch_shapes=[W_SCRATCH, pltpu.SemaphoreType.DMA],
        ),
        out_shape=jax.ShapeDtypeStruct((2, TOKENS, COLS), f32),
        compiler_params=params(),
        cost_estimate=COST,
        name="project_first",
    )(place, *[own] * 4, *[partner] * 4, *weights)


def second_call(place, facts, own, partner, weights, sums, cot, scales, k_gain):
    whole = pl.BlockSpec((SEQS, 2, ROWS, COLS), lambda i, *s: (0, 0, 0, 0))
    cots = pl.BlockSpec((SEQS, 2, ROWS + EXTRA, COLS), lambda i, *s: (0, 0, 0, 0))
    wide = pl.BlockSpec((STEP, HEAD), lambda i, *s: (i, 0))
    return pl.pallas_call(
        second_kernel,
        grid_spec=pltpu.PrefetchScalarGridSpec(
            num_scalar_prefetch=2,
            grid=(TOKENS // STEP,),
            in_specs=token_specs(other_pair)
            + [ANY_SPEC] * 2
            + [SUM_SPEC, cots, wide, wide]
            + [pl.BlockSpec((1, HEAD), lambda i, *s: (0, 0))],
            out_specs=[whole, SUM_SPEC],
            scratch_shapes=[W_SCRATCH, pltpu.VMEM((2, STEP, COLS), f32), pltpu.SemaphoreType.DMA],
        ),
        out_shape=[
            jax.ShapeDtypeStruct((SEQS, 2, ROWS, COLS), bf16),
            jax.ShapeDtypeStruct((2, TOKENS, COLS), bf16),
        ],
        compiler_params=params(45),
        cost_estimate=COST,
        name="project_second",
    )(
        place, facts, *[own] * 4, *[partner] * 4, *weights, sums, cot, *scales,
        k_gain.reshape(1, HEAD),
    )


def gradient_kernel(place, own_ref, partner_ref, scaled_ref, same_ref, cross_ref):
    core, u, v = place[0], place[1], place[2]
    j = pl.program_id(0)
    total = None
    for side, ref in enumerate((own_ref, partner_ref)):
        part = lax.dot_general(
            ref[...].reshape(TOKENS, PAIR),
            scaled_ref[side],
            (((0,), (0,)), ((), ())),
            preferred_element_type=f32,
        )
        total = part if total is None else total + part
    total = total.astype(bf16)
    for s in range(2):
        bit = jnp.where(core == 0, lax.div(j, 2), s)
        vv = jnp.where(core == 0, 2 * lax.rem(j, 2) + s, j)
        n = lax.bitwise_xor(vv, v)
        rows = total[s * BLOCK : (s + 1) * BLOCK]
        same = bit == lax.rem(u, 2)

        @pl.when(same)
        def _():
            same_ref[n] = rows

        @pl.when(jnp.logical_not(same))
        def _():
            cross_ref[n] = rows


def gradient_call(pair_of, place, own, partner, scaled):
    tokens = pl.BlockSpec((SEQS, ROWS, PAIR), lambda j, p: (0, 0, window(pair_of, j, p)))
    out = pl.BlockSpec((4, BLOCK, COLS), lambda j, p: (0, 0, 0))
    return pl.pallas_call(
        gradient_kernel,
        grid_spec=pltpu.PrefetchScalarGridSpec(
            num_scalar_prefetch=1,
            grid=(4,),
            in_specs=[tokens, tokens, pl.BlockSpec((2, TOKENS, COLS), lambda j, p: (0, 0, 0))],
            out_specs=[out, out],
        ),
        out_shape=[jax.ShapeDtypeStruct((4, BLOCK, COLS), bf16)] * 2,
        compiler_params=params(),
        cost_estimate=COST,
        name="weight_gradient",
    )(place, own, partner, scaled)


def sums_kernel(rewards_ref, groups_ref, sums_ref):
    lane = lax.broadcasted_iota(jnp.int32, (1, 2 * GROUPS), 1)
    total = jnp.zeros((1, 2 * GROUPS), jnp.int32)
    for n in range(SEQS):
        reward, group = rewards_ref[n], groups_ref[n]
        total += jnp.where(lane == group, reward, 0)
        total += jnp.where(lane == group + GROUPS, reward * reward, 0)
    sums_ref[...] = total.astype(f32)


def group_sums(rewards, group_ids):
    return pl.pallas_call(
        sums_kernel,
        in_specs=[pl.BlockSpec(memory_space=pltpu.SMEM)] * 2,
        out_specs=pl.BlockSpec(memory_space=pltpu.VMEM),
        out_shape=jax.ShapeDtypeStruct((1, 2 * GROUPS), f32),
        cost_estimate=COST,
        name="group_sums",
    )(rewards, group_ids)


def as_rows(sums):
    return jnp.pad(sums.astype(bf16), ((0, EXTRA - 1), (0, COLS - 2 * GROUPS)))


def columns_of(core, array):
    k0, k1, v0, v1 = (array[..., i * HALF : (i + 1) * HALF] for i in range(4))
    return jnp.where(
        core == 0, jnp.concatenate([k0, v0], -1), jnp.concatenate([k1, v1], -1)
    )


def all_columns(core, mine, other):
    low, high = jnp.where(core == 0, mine, other), jnp.where(core == 0, other, mine)
    return jnp.concatenate(
        [low[..., :HALF], high[..., :HALF], low[..., HALF:], high[..., HALF:]], -1
    )


def on_device(
    hidden_in, kv_weight, ln_gain, k_gain, cost_slots, lengths, rewards, group_ids, kv_cotangent
):
    place_f = lax.axis_index("fsdp")
    core = lax.rem(lax.axis_index("dp"), 2)
    y, z = lax.div(place_f, 4), lax.rem(place_f, 4)
    place = jnp.stack([core, jnp.where(core == 0, y, z), jnp.where(core == 0, z, y)])
    place = place.astype(jnp.int32)
    gain = lax.dynamic_slice(ln_gain, (place_f * BLOCK,), (BLOCK,))[:, None]

    facts = jnp.stack([cost_slots[0], lengths, rewards, group_ids])
    facts = jnp.concatenate([facts, to_partner(facts)])

    mine = (columns_of(core, kv_weight).astype(f32) * gain).astype(bf16)
    sums = group_sums(rewards, group_ids)
    sums = sums + sum(along(sums, True, m) for m in (1, 2, 3))
    mine = jnp.concatenate([mine, as_rows(sums)])
    blocks = [mine] + [along(mine, False, n) for n in (1, 2, 3)]
    piece = jnp.concatenate([block[:BLOCK] for block in blocks])
    pieces = [piece] + [along(piece, True, m) for m in (1, 2, 3)]

    totals = sum(block[BLOCK : BLOCK + 1, : 2 * GROUPS].astype(f32) for block in blocks)

    k0, k1, v0, v1 = (
        kv_cotangent[..., i * HALF : (i + 1) * HALF].reshape(4, 2, ROWS, HALF) for i in range(4)
    )
    cot = jnp.stack([jnp.concatenate([k0, v0], -1), jnp.concatenate([k1, v1], -1)], 1)
    totals = jnp.broadcast_to(as_rows(totals), (SEQS, 2, EXTRA, COLS))
    cot = jnp.concatenate([cot.reshape(SEQS, 2, ROWS, COLS), totals], 2)
    cot = lax.all_to_all(cot, "dp", split_axis=0, concat_axis=0, tiled=True)

    swapped, _ = lax.optimization_barrier((hidden_in, piece))
    partner = to_partner(swapped)

    scale = scale_call(hidden_in)

    scales = scale, to_partner(scale)
    sums = first_call(place, hidden_in, partner, pieces[:2])
    kv, scaled = second_call(
        place, facts, hidden_in, partner, pieces[2:], sums, cot, scales, k_gain
    )
    kv = lax.all_to_all(kv, "dp", split_axis=0, concat_axis=0, tiled=True)

    two, three = gradient_call(other_pair, place, hidden_in, partner, scaled)
    here, one = gradient_call(own_pair, place, hidden_in, partner, scaled)
    received = [here, along(two, True, 2), along(three, True, 3), along(one, True, 1)]
    total = None
    for n in (2, 1, 3, 0):
        block = sum(part[n].astype(f32) for part in received)
        if n:
            received = lax.optimization_barrier(received)
            block = along(block.astype(bf16), False, n).astype(f32)
        total = block if total is None else total + block
    rows = total.astype(bf16)
    kv, rows = lax.optimization_barrier((kv, rows))
    kv = kv.reshape(4, 2, 2, ROWS, COLS)
    low, high = kv[:, 0], jnp.stack([kv[:, 1, 1], kv[:, 1, 0]], 1)
    keys_values = jnp.concatenate(
        [low[..., :HALF], high[..., :HALF], low[..., HALF:], high[..., HALF:]], -1
    ).reshape(SEQS, ROWS, 2 * COLS)
    ring = [rows.astype(f32)] + [along_x(rows, k).astype(f32) for k in (1, 2, 3)]
    rows = ((ring[0] + ring[2]) + (ring[1] + ring[3])) * gain
    rows, keys_values = lax.optimization_barrier((rows, keys_values))
    return keys_values, all_columns(core, rows, to_partner(rows))


def solution(mesh):
    in_specs = (
        P(("dp", "fsdp"), None, None),
        P("fsdp", None),
        P(),
        P(),
        P(("dp", "fsdp"), None),
        P(("dp", "fsdp")),
        P(("dp", "fsdp")),
        P(("dp", "fsdp")),
        P(("dp", "fsdp"), None, None),
    )
    out_specs = (P(("dp", "fsdp"), None, None), P("fsdp", None))
    return jax.shard_map(
        on_device, mesh=mesh, in_specs=in_specs, out_specs=out_specs, check_vma=False
    )
```
